256 devices in a mesh: chan: 16 (over x_lo, z), bl: 16 (over y, x_hi, core).
Axes of the slice: x: 4 (x_hi: 2, x_lo: 2; x = x_hi * 2 + x_lo), y: 4, z: 8, core: 2. Of those that a mesh axis runs over, the one named last changes fastest.
Arguments:
- visibility: float32 [2, 2, 256, 8192], P(None, None, 'chan', 'bl'), may hold values from -12 to 12
- coherency: float32 [2, 2, 16, 256, 8192], P(None, None, None, 'chan', 'bl'), may hold values from -6 to 6
- station_pairs: int32 [2, 8192], P(None, 'bl'), may hold values from 0 to 511, as said below
- jones_gains: float32 [2, 2, 16, 256, 512], P(None, None, None, 'chan', 'bl'), may hold values from -1.2 to 2.2
- scaled_duals: float32 [2, 2, 16, 256, 512], P(None, None, None, 'chan', 'bl'), may hold values from -1.8 to 1.8
- penalty: float32 [16], replicated, may hold values from 5 to 50
Outputs:
- jones_out: float32 [2, 2, 16, 256, 512], P(None, None, None, 'chan', 'bl')
- duals_out: float32 [2, 2, 16, 256, 512], P(None, None, None, 'chan', 'bl')
The draws below stay inside these ranges and needn't reach their ends.
Inputs may be any that keep to these rules, and one draw needn't show every extreme that they name: `station_pairs`: each row names two different stations.
All inputs are finite; a program needn't handle non-finite values.
Results may differ from the reference program's by a relative error of at most 0.00014.
Values sent between devices are 32-bit elements; how exact they have to be, the bound alone decides.
A program may use at most 128 MiB of HBM per device.

```python
import math
import jax
import jax.numpy as jnp
from jax import lax

STATION_COUNT = 512
CAL_DIRECTIONS = 16
FREQ_CHANNELS = 256
ITERS = 2
NPOLY = 3
BASELINE_ROWS = 8192


def draw_station_pairs(key, part):
    key = jax.random.fold_in(key, 12)
    leading_key, iteration_key = jax.random.split(key)
    leading_station = jax.random.randint(leading_key, (BASELINE_ROWS,), 0, STATION_COUNT, dtype=jnp.int32)
    row_offset = jax.random.randint(iteration_key, (BASELINE_ROWS,), 1, STATION_COUNT, dtype=jnp.int32)
    second = (leading_station + row_offset) % STATION_COUNT
    return jnp.stack([leading_station, second]).astype(jnp.int32)


def draw_jones_gains(key, part):
    key = jax.random.fold_in(key, 11)
    shape = (2, 2, CAL_DIRECTIONS, FREQ_CHANNELS, STATION_COUNT)
    noise = jnp.clip(0.3 * jax.random.normal(key, shape, jnp.float32), -1.2, 1.2)
    centre = (lax.broadcasted_iota(jnp.int32, shape, 0) == 0).astype(jnp.float32)
    return noise + centre


def levels(key, dims, shards, smallest, high):
    level, own = 1.0, jax.random.fold_in(key, 6)
    for position, parts in shards:
        draws = jnp.exp(jax.random.uniform(jax.random.fold_in(own, position), (parts,), jnp.float32, smallest / len(shards), high / len(shards)))
        level = level * jnp.repeat(draws, dims[position] // parts).reshape([-1 if axis == position else 1 for axis in range(len(dims))])
    return level


def scatter_about(stream_key, shape, scale, reach, cuts=(), held_as=jnp.bfloat16):
    factor_of = levels(stream_key, shape, cuts, -0.22, 0.18) if cuts else 1.0
    values = jax.random.normal(stream_key, shape, jnp.float32) * scale * factor_of
    return jnp.minimum(jnp.maximum(values, -reach), reach).astype(held_as)


def setup_inputs(seed: int = 0) -> dict:
    key_of = jax.random.split(jax.random.key(seed), 7)
    return {
        "visibility": scatter_about(key_of[0], (2, 2, FREQ_CHANNELS, BASELINE_ROWS), 2.0, 12.0, ((2, 16), (3, 16)), jnp.float32),
        "coherency": scatter_about(key_of[1], (2, 2, CAL_DIRECTIONS, FREQ_CHANNELS, BASELINE_ROWS), 1.0, 6.0, ((3, 16), (4, 16)), jnp.float32),
        "station_pairs": draw_station_pairs(jax.random.fold_in(key_of[6], 71), 0),
        "jones_gains": draw_jones_gains(jax.random.fold_in(key_of[6], 71), 0),
        "scaled_duals": scatter_about(key_of[4], (2, 2, CAL_DIRECTIONS, FREQ_CHANNELS, STATION_COUNT), 0.3, 1.8, ((3, 16), (4, 16)), jnp.float32),
        "penalty": jnp.clip(jnp.exp(jax.random.uniform(key_of[5], (CAL_DIRECTIONS,), jnp.float32, math.log(5.0), math.log(50.0))), 5.0, 50.0),
    }


def cosine_table(first_channel, channel_count):
    freq = (first_channel + lax.broadcasted_iota(jnp.int32, (channel_count, NPOLY), 0)).astype(jnp.float32)
    order = lax.broadcasted_iota(jnp.int32, (channel_count, NPOLY), 1).astype(jnp.float32)
    scale = jnp.where(order < 0.5, math.sqrt(1.0 / FREQ_CHANNELS), math.sqrt(2.0 / FREQ_CHANNELS))
    return scale * jnp.cos(math.pi * order * (freq + 0.5) / FREQ_CHANNELS)

def fit_terms(basis_table, target):
    return jnp.einsum('fb,rpkfs->rpkbs', basis_table, target, precision=lax.Precision.HIGHEST)

def spread_terms(basis_table, coeff):
    return jnp.einsum('fb,rpkbs->rpkfs', basis_table, coeff, precision=lax.Precision.HIGHEST)

def normal_terms(vis_data, coh_data, paired):
    row_count = vis_data.shape[-1]
    left_gain = paired[..., :row_count]
    right_gain = paired[..., row_count:]
    prod_re = left_gain[0] * coh_data[0] - left_gain[1] * coh_data[1]
    prod_im = left_gain[0] * coh_data[1] + left_gain[1] * coh_data[0]
    model_re = prod_re * right_gain[0] + prod_im * right_gain[1]
    model_im = prod_im * right_gain[0] - prod_re * right_gain[1]
    resid_re = (vis_data[0] - lax.optimization_barrier(jnp.sum(model_re, axis=1)))[:, None]
    resid_im = (vis_data[1] - lax.optimization_barrier(jnp.sum(model_im, axis=1)))[:, None]
    side_re = coh_data[0] * right_gain[0] + coh_data[1] * right_gain[1]
    side_im = coh_data[1] * right_gain[0] - coh_data[0] * right_gain[1]
    first_re = resid_re * side_re + resid_im * side_im
    first_im = resid_im * side_re - resid_re * side_im
    second_re = resid_re * prod_re + resid_im * prod_im
    second_im = resid_re * prod_im - resid_im * prod_re
    first_wt = side_re * side_re + side_im * side_im
    second_wt = prod_re * prod_re + prod_im * prod_im
    return jnp.stack([jnp.concatenate([first_re, second_re], axis=-1), jnp.concatenate([first_im, second_im], axis=-1), jnp.concatenate([first_wt, second_wt], axis=-1)])

def advance(gain_state, dual_state, fitted, sums, penalty):
    weight = penalty[:, None, None]
    gain_state = gain_state + (sums[0:2] + weight * (fitted - dual_state - gain_state)) / (sums[2][None] + weight)
    dual_state = dual_state + gain_state - fitted
    return (gain_state, dual_state)

def reference(visibility, coherency, station_pairs, jones_gains, scaled_duals, penalty):
    basis_table = cosine_table(0, FREQ_CHANNELS)
    station_ids = jnp.concatenate([station_pairs[0], station_pairs[1]]).astype(jnp.int32)
    vis_chan = jnp.moveaxis(visibility, 2, 0)
    coh_chan = jnp.moveaxis(coherency, 3, 0)
    gain_state, dual_state = (jones_gains, scaled_duals)

    def per_channel(items):
        vis_one, coh_one, gain_one = items
        paired = jnp.concatenate([jnp.take(gain_one, station_pairs[0].astype(jnp.int32), axis=3), jnp.take(gain_one, station_pairs[1].astype(jnp.int32), axis=3)], axis=3)
        contrib = normal_terms(vis_one, coh_one, paired)
        summed = jax.ops.segment_sum(jnp.moveaxis(contrib, -1, 0), station_ids, num_segments=STATION_COUNT)
        return jnp.moveaxis(summed, 0, -1)
    for iteration in range(ITERS):
        coeff = fit_terms(basis_table, gain_state + dual_state)
        fitted = spread_terms(basis_table, coeff)
        sums = lax.map(per_channel, (vis_chan, coh_chan, jnp.moveaxis(gain_state, 3, 0)))
        sums = jnp.moveaxis(sums, 0, 3)
        gain_state, dual_state = advance(gain_state, dual_state, fitted, sums, penalty)
    return (gain_state, dual_state)
```

```python
import functools
import math

import jax
import jax.numpy as jnp
import numpy as np
from jax import lax
from jax.experimental import pallas as pl
from jax.experimental.pallas import tpu as pltpu
from jax.sharding import PartitionSpec as P

STATIONS = 512
CHANNELS = 256
NPOLY = 3
DIRS = 16
GROUP = 16
ROWS = 512
OWN = STATIONS // GROUP
HALF = 256
MESH = pl.DeviceIdType.MESH
f32, bf16 = jnp.float32, jnp.bfloat16


def cosine_table():
    freq = np.arange(CHANNELS, dtype=np.float64)[:, None]
    order = np.arange(NPOLY, dtype=np.float64)[None, :]
    scale = np.where(order < 0.5, math.sqrt(1.0 / CHANNELS), math.sqrt(2.0 / CHANNELS))
    return (scale * np.cos(math.pi * order * (freq + 0.5) / CHANNELS)).astype(np.float32)


def split(x):
    hi = x.astype(bf16)
    return hi, (x - hi.astype(f32)).astype(bf16)


def regroup(blocks):
    lane = lax.broadcasted_iota(jnp.int32, blocks[0].shape, 1) // OWN
    outs = []
    for i in range(4):
        out = None
        for a, block in enumerate(blocks):
            shift = (OWN * (a - i)) % 128
            moved = pltpu.roll(block, shift, 1) if shift else block
            out = moved if out is None else jnp.where(lane == a, moved, out)
        outs.append(out)
    return outs


def build_onehot(c_ref, oh_ref, b):
    station = lax.broadcasted_iota(jnp.int32, (HALF, ROWS), 0).astype(f32)
    for side in range(2):
        pair = c_ref[b, 68 + side : 69 + side, :]
        low = jnp.where(pair >= HALF, pair - HALF, pair)
        oh_ref[b, :, side * ROWS : (side + 1) * ROWS] = jnp.where(station == low, 1.0, 0.0).astype(bf16)


def set_table(g_ref, gcat_ref):
    for row in range(0, 64, 16):
        for half in range(2):
            hi, lo = split(g_ref[row : row + 16, half * HALF : (half + 1) * HALF])
            gcat_ref[half * 128 + row : half * 128 + row + 16, :] = hi
            gcat_ref[half * 128 + 64 + row : half * 128 + 80 + row, :] = lo


def row_terms(c_ref, x_ref, s_ref, b, n=128):
    for l in range(0, ROWS, n):
        upper = [
            jnp.broadcast_to(c_ref[b, 68 + side : 69 + side, l : l + n] >= HALF, (DIRS, n))
            for side in range(2)
        ]
        for pol in range(2):

            def gain(side, part):
                o = part * 32 + pol * 16
                at = slice(side * ROWS + l, side * ROWS + l + n)
                h0, l0, h1, l1 = [x_ref[k + o : k + o + 16, at] for k in (0, 64, 128, 192)]
                return jnp.where(upper[side], h1, h0) + jnp.where(upper[side], l1, l0)

            pr, pi, qr, qi = gain(0, 0), gain(0, 1), gain(1, 0), gain(1, 1)
            cr = c_ref[b, 16 * pol : 16 * pol + 16, l : l + n]
            ci = c_ref[b, 32 + 16 * pol : 48 + 16 * pol, l : l + n]
            dr = pr * cr - pi * ci
            di = pr * ci + pi * cr
            mr = dr * qr + di * qi
            mi = di * qr - dr * qi
            rr = c_ref[b, 64 + pol : 65 + pol, l : l + n] - jnp.sum(mr, axis=0, keepdims=True)
            ri = c_ref[b, 66 + pol : 67 + pol, l : l + n] - jnp.sum(mi, axis=0, keepdims=True)
            sr = cr * qr + ci * qi
            si = ci * qr - cr * qi
            first = (rr * sr + ri * si, ri * sr - rr * si, sr * sr + si * si)
            second = (rr * dr + ri * di, rr * di - ri * dr, dr * dr + di * di)
            for side, terms in enumerate((first, second)):
                for comp, term in enumerate(terms):
                    for half in range(2):
                        if half:
                            kept = jnp.where(upper[side], term, 0.0)
                        else:
                            kept = jnp.where(upper[side], 0.0, term)
                        hi, lo = split(kept)
                        o = half * 192 + comp * 32 + pol * 16
                        at = slice(side * ROWS + l, side * ROWS + l + n)
                        s_ref[o : o + 16, at] = hi
                        s_ref[o + 96 : o + 112, at] = lo


def kernel(
    coh, vis, pairs, jones, duals, pen, table,
    jones_out, duals_out,
    raw, vraw, cown, C, J, U, J1, S2, g_ref, u_own, usend, j1send, s2send, coef, xbuf, zbuf,
    oh, gcat, x_ref, s_ref, acc,
    ssem, rsem, lsem, cs, cr,
):
    ch = lax.axis_index("chan")
    me = lax.axis_index("bl")
    y, x, c = me // 4, (me // 2) % 2, me % 2
    xl, z = ch // 8, ch % 8

    def to(o):
        return ((y + o // 4) % 4) * 4 + ((x + (o // 2) % 2) % 2) * 2 + (c + o % 2) % 2

    def fro(o):
        return ((y + 4 - o // 4) % 4) * 4 + ((x + (o // 2) % 2) % 2) * 2 + (c + o % 2) % 2

    def xpeer():
        return {"chan": (1 - xl) * 8 + z}

    def zpeer(o):
        return {"chan": xl * 8 + (z + o) % 8}

    barrier = pltpu.get_barrier_semaphore()

    @pl.loop(1, GROUP)
    def _(o):
        pl.semaphore_signal(barrier, inc=1, device_id={"bl": to(o)}, device_id_type=MESH)

    pl.semaphore_signal(barrier, inc=1, device_id=xpeer(), device_id_type=MESH)

    @pl.loop(1, 8)
    def _(o):
        pl.semaphore_signal(barrier, inc=1, device_id=zpeer(o), device_id_type=MESH)

    mine = [
        pltpu.make_async_copy(
            src.at[:, pl.ds(128 * t, 128)], dst.at[pl.ds(t * deep, deep)], lsem.at[i, t]
        )
        for t in range(ROWS // 128)
        for i, (src, dst, deep) in enumerate(((coh, raw, 64 * GROUP), (vis, vraw, 4 * GROUP)))
    ]
    for copy in mine:
        copy.start()
    J[me] = jones[me]
    fill = jnp.concatenate([pairs[...].astype(f32), jnp.zeros((2, ROWS), f32)], axis=0)
    for copy in mine:
        copy.wait()

    @pl.loop(0, GROUP)
    def _(f):
        for t in range(ROWS // 128):
            at = slice(128 * t, 128 * t + 128)
            for k in range(0, 64, 8):
                cown[f, k : k + 8, at] = raw[pl.ds(f + (64 * t + k) * GROUP, 8, stride=GROUP)]
            cown[f, 64:68, at] = vraw[pl.ds(f + 4 * t * GROUP, 4, stride=GROUP)]
        cown[f, 68:72] = fill

    C[me] = cown[me]
    pl.semaphore_wait(barrier, 23)

    def remote(kind, o, src, dst):
        return pltpu.make_async_remote_copy(
            src_ref=src, dst_ref=dst, send_sem=ssem.at[kind, o], recv_sem=rsem.at[kind, o],
            device_id={"bl": to(o)}, device_id_type=MESH,
        )

    def jones_to(o):
        return remote(0, o, jones.at[to(o)], J.at[me])

    def coh_to(o):
        return remote(1, o, cown.at[to(o)], C.at[me])

    def u_to(o):
        return remote(2, o, usend.at[to(o)], U.at[me])

    def j1_to(o):
        return remote(3, o, j1send.at[to(o)], J1.at[me])

    def s2_to(o):
        return remote(4, o, s2send.at[to(o)], S2.at[me])

    def x_copy(it):
        return pltpu.make_async_remote_copy(
            src_ref=coef.at[2 * it], dst_ref=xbuf.at[it], send_sem=cs.at[it, 0], recv_sem=cr.at[it, 0],
            device_id=xpeer(), device_id_type=MESH,
        )

    def z_copy(it, o):
        return pltpu.make_async_remote_copy(
            src_ref=coef.at[2 * it + 1], dst_ref=zbuf.at[it, o], send_sem=cs.at[it, o], recv_sem=cr.at[it, o],
            device_id=zpeer(o), device_id_type=MESH,
        )

    @pl.loop(1, GROUP)
    def _(o):
        jones_to(o).start()

    @pl.loop(1, GROUP)
    def _(o):
        coh_to(o).start()

    def basis(f, b):
        return table[(ch * GROUP + f) * NPOLY + b]

    def fit(it, target):
        total = [jnp.zeros((DIRS, 128), f32) for _ in range(NPOLY)]
        for f in range(GROUP):
            value = target(f)
            for b in range(NPOLY):
                total[b] += basis(f, b) * value
        for b in range(NPOLY):
            coef[2 * it, b] = total[b]
        x_copy(it).start()

    def fit_x(it):
        x_copy(it).wait_recv()
        coef[2 * it + 1] = coef[2 * it] + xbuf[it]

        @pl.loop(1, 8)
        def _(o):
            z_copy(it, o).start()

    def fit_z(it):
        @pl.loop(1, 8)
        def _(o):
            z_copy(it, o).wait_recv()

        total = [coef[2 * it + 1, b] for b in range(NPOLY)]
        for o in range(1, 8):
            for b in range(NPOLY):
                total[b] += zbuf[it, o, b]

        def fitted(f):
            return sum(basis(f, b) * total[b] for b in range(NPOLY))

        return fitted

    fit(0, lambda f: jones[f] + duals[f])
    fit_x(0)
    fitted = fit_z(0)
    for f in range(GROUP):
        u_own[f] = fitted(f) - duals[f]
    usend[...] = u_own[...]
    U[me] = u_own[me]

    @pl.loop(1, GROUP)
    def _(o):
        u_to(o).start()


    @pl.loop(1, GROUP)
    def _(o):
        jones_to(o).wait_recv()

    for q in range(4):
        for a, block in enumerate(regroup([J[4 * q + i] for i in range(4)])):
            g_ref[16 * a : 16 * a + 16, 128 * q : 128 * q + 128] = block
    set_table(g_ref, gcat)
    acc[...] = jnp.zeros_like(acc)

    def block(b):
        x_ref[...] = jnp.dot(gcat[...], oh[b], preferred_element_type=f32)
        row_terms(C, x_ref, s_ref, b)
        acc[...] += lax.dot_general(
            s_ref[...], oh[b], (((1,), (1,)), ((), ())), preferred_element_type=f32
        )

    @pl.loop(0, GROUP)
    def _(o):
        b = fro(o)

        @pl.when(o > 0)
        def _():
            coh_to(o).wait_recv()

        build_onehot(C, oh, b)
        block(b)

    def sums(comp, pol, q):
        o, at = (q // 2) * 192 + comp * 32 + pol * 16, slice((q % 2) * 128, (q % 2) * 128 + 128)
        return acc[o : o + 16, at] + acc[o + 96 : o + 112, at]

    row = lax.broadcasted_iota(jnp.int32, (DIRS, 128), 0)
    weight = jnp.zeros((DIRS, 128), f32)
    for k in range(DIRS):
        weight = jnp.where(row == k, pen[k], weight)

    @pl.loop(1, GROUP)
    def _(o):
        u_to(o).wait_recv()

    for q in range(4):
        u = regroup([U[4 * q + i] for i in range(4)])
        wide = [sums(2, pol, q) + weight for pol in range(2)]
        new = []
        for a in range(4):
            gain = g_ref[16 * a : 16 * a + 16, 128 * q : 128 * q + 128]
            gain = gain + (sums(a // 2, a % 2, q) + weight * (u[a] - gain)) / wide[a % 2]
            g_ref[16 * a : 16 * a + 16, 128 * q : 128 * q + 128] = gain
            new.append(gain)
        for i, slab in enumerate(regroup(new)):
            j1send[4 * q + i] = slab
    J1[me] = j1send[me]

    @pl.loop(1, GROUP)
    def _(o):
        j1_to(o).start()

    set_table(g_ref, gcat)
    acc[...] = jnp.zeros_like(acc)

    @pl.loop(0, 4)
    def _(o):
        block(o)

    @pl.loop(1, GROUP)
    def _(o):
        j1_to(o).wait_recv()

    fit(1, lambda f: 2.0 * J1[f] - u_own[f])

    @pl.loop(4, 8)
    def _(o):
        block(o)

    fit_x(1)

    @pl.loop(8, 14)
    def _(o):
        block(o)

    fitted = fit_z(1)
    for f in range(GROUP):
        u_own[f] = fitted(f) - (J1[f] - u_own[f])

    @pl.loop(14, 16)
    def _(o):
        block(o)

    for q in range(4):
        grads = regroup([sums(a // 2, a % 2, q) for a in range(4)])
        wides = [sums(2, pol, q) for pol in range(2)]
        wides = regroup([wides[a % 2][8 * (a // 2) : 8 * (a // 2) + 8] for a in range(4)])
        for i in range(4):
            s2send[4 * q + i, 0:16] = grads[i]
            s2send[4 * q + i, 16:24] = wides[i]
    S2[me] = s2send[me]

    @pl.loop(1, GROUP)
    def _(o):
        s2_to(o).start()

    @pl.loop(1, GROUP)
    def _(o):
        s2_to(o).wait_recv()

    low = lax.broadcasted_iota(jnp.int32, (8, 128), 1) < 64
    for f in range(GROUP):
        packed = S2[f, 16:24]
        turned = pltpu.roll(packed, 64, 1)
        for h, wide in enumerate((jnp.where(low, packed, turned), jnp.where(low, turned, packed))):
            at = slice(8 * h, 8 * h + 8)
            gain, u, pk = J1[f, at], u_own[f, at], weight[at]
            gain = gain + (S2[f, at] + pk * (u - gain)) / (wide + pk)
            jones_out[f, at] = gain
            duals_out[f, at] = gain - u

    @pl.loop(1, GROUP)
    def _(o):
        for copy in (jones_to, coh_to, u_to, j1_to, s2_to):
            copy(o).wait_send()

    for it in range(2):
        x_copy(it).wait_send()

        @pl.loop(1, 8)
        def _(o):
            z_copy(it, o).wait_send()


def body(visibility, coherency, station_pairs, jones_gains, scaled_duals, penalty):
    def pack(state):
        return jnp.transpose(state, (3, 2, 0, 1, 4)).reshape(GROUP, DIRS, 128)

    def unpack(state):
        return jnp.transpose(state.reshape(GROUP, DIRS, 2, 2, OWN), (2, 3, 1, 0, 4))

    slab = (GROUP, DIRS, 128)
    out = jax.ShapeDtypeStruct(slab, f32)
    hbm, vmem, smem = [
        pl.BlockSpec(memory_space=space) for space in (pltpu.HBM, pltpu.VMEM, pltpu.SMEM)
    ]
    jones, duals = pl.pallas_call(
        kernel,
        out_shape=(out, out),
        in_specs=[hbm, hbm, vmem, vmem, vmem, smem, smem],
        out_specs=(vmem, vmem),
        scratch_shapes=[
            pltpu.VMEM((4 * 64 * GROUP, 128), f32),
            pltpu.VMEM((4 * 4 * GROUP, 128), f32),
            pltpu.VMEM((GROUP, 72, ROWS), f32),
            pltpu.VMEM((GROUP, 72, ROWS), f32),
            pltpu.VMEM(slab, f32),
            pltpu.VMEM(slab, f32),
            pltpu.VMEM(slab, f32),
            pltpu.VMEM((GROUP, 24, 128), f32),
            pltpu.VMEM((64, STATIONS), f32),
            pltpu.VMEM(slab, f32),
            pltpu.VMEM(slab, f32),
            pltpu.VMEM(slab, f32),
            pltpu.VMEM((GROUP, 24, 128), f32),
            pltpu.VMEM((4, NPOLY, DIRS, 128), f32),
            pltpu.VMEM((2, NPOLY, DIRS, 128), f32),
            pltpu.VMEM((2, 8, NPOLY, DIRS, 128), f32),
            pltpu.VMEM((GROUP, HALF, 2 * ROWS), bf16),
            pltpu.VMEM((256, HALF), bf16),
            pltpu.VMEM((256, 2 * ROWS), f32),
            pltpu.VMEM((384, 2 * ROWS), bf16),
            pltpu.VMEM((384, HALF), f32),
            pltpu.SemaphoreType.DMA((5, GROUP)),
            pltpu.SemaphoreType.DMA((5, GROUP)),
            pltpu.SemaphoreType.DMA((2, 4)),
            pltpu.SemaphoreType.DMA((2, 8)),
            pltpu.SemaphoreType.DMA((2, 8)),
        ],
        compiler_params=pltpu.CompilerParams(
            collective_id=0, has_side_effects=True, vmem_limit_bytes=48 * 2**20
        ),
    )(
        coherency.reshape(64 * GROUP, ROWS),
        visibility.reshape(4 * GROUP, ROWS),
        station_pairs,
        pack(jones_gains),
        pack(scaled_duals),
        penalty,
        jnp.asarray(cosine_table().reshape(-1)),
    )
    return unpack(jones), unpack(duals)


def solution(mesh):
    state = P(None, None, None, "chan", "bl")
    return jax.shard_map(
        body,
        mesh=mesh,
        in_specs=(P(None, None, "chan", "bl"), state, P(None, "bl"), state, state, P()),
        out_specs=(state, state),
        check_vma=False,
    )
```

```python
import functools
import math

import jax
import jax.numpy as jnp
import numpy as np
from jax import lax
from jax.experimental import pallas as pl
from jax.experimental.pallas import tpu as pltpu
from jax.sharding import PartitionSpec as P

STATIONS = 512
CHANNELS = 256
NPOLY = 3
DIRS = 16
GROUP = 16
ROWS = 512
OWN = STATIONS // GROUP
HALF = 256
LOGICAL = pl.DeviceIdType.LOGICAL
ZORDER = (1, 7, 2, 6, 3, 5, 4)
f32, bf16 = jnp.float32, jnp.bfloat16


def cosine_table():
    freq = np.arange(CHANNELS, dtype=np.float64)[:, None]
    order = np.arange(NPOLY, dtype=np.float64)[None, :]
    scale = np.where(order < 0.5, math.sqrt(1.0 / CHANNELS), math.sqrt(2.0 / CHANNELS))
    return (scale * np.cos(math.pi * order * (freq + 0.5) / CHANNELS)).astype(np.float32)


def split(x):
    hi = x.astype(bf16)
    return hi, (x - hi.astype(f32)).astype(bf16)


def regroup(blocks):
    lane = lax.broadcasted_iota(jnp.int32, blocks[0].shape, 1) // OWN
    outs = []
    for i in range(4):
        out = None
        for a, block in enumerate(blocks):
            shift = (OWN * (a - i)) % 128
            moved = pltpu.roll(block, shift, 1) if shift else block
            out = moved if out is None else jnp.where(lane == a, moved, out)
        outs.append(out)
    return outs


def build_onehot(j_ref, oh_ref, b):
    station = lax.broadcasted_iota(jnp.int32, (HALF, 128), 0).astype(f32)
    for k in range(8):
        pair = j_ref[b, DIRS + k : DIRS + k + 1, :]
        low = jnp.where(pair >= HALF, pair - HALF, pair)
        oh_ref[b, :, 128 * k : 128 * k + 128] = jnp.where(station == low, 1.0, 0.0).astype(bf16)


def set_table(g_ref, gcat_ref):
    for row in range(0, 64, 16):
        for half in range(2):
            hi, lo = split(g_ref[row : row + 16, half * HALF : (half + 1) * HALF])
            gcat_ref[half * 128 + row : half * 128 + row + 16, :] = hi
            gcat_ref[half * 128 + 64 + row : half * 128 + 80 + row, :] = lo


def row_terms(c_ref, j_ref, x_ref, s_ref, b, n=128):
    for l in range(0, ROWS, n):
        upper = [
            jnp.broadcast_to(j_ref[b, pl.ds(DIRS + 4 * side + l // n, 1), :] >= HALF, (DIRS, n))
            for side in range(2)
        ]
        for pol in range(2):

            def gain(side, part):
                o = part * 32 + pol * 16
                at = slice(side * ROWS + l, side * ROWS + l + n)
                h0, l0, h1, l1 = [x_ref[k + o : k + o + 16, at] for k in (0, 64, 128, 192)]
                return jnp.where(upper[side], h1, h0) + jnp.where(upper[side], l1, l0)

            pr, pi, qr, qi = gain(0, 0), gain(0, 1), gain(1, 0), gain(1, 1)
            cr = c_ref[b, 16 * pol : 16 * pol + 16, l : l + n]
            ci = c_ref[b, 32 + 16 * pol : 48 + 16 * pol, l : l + n]
            dr = pr * cr - pi * ci
            di = pr * ci + pi * cr
            mr = dr * qr + di * qi
            mi = di * qr - dr * qi
            rr = c_ref[b, 64 + pol : 65 + pol, l : l + n] - jnp.sum(mr, axis=0, keepdims=True)
            ri = c_ref[b, 66 + pol : 67 + pol, l : l + n] - jnp.sum(mi, axis=0, keepdims=True)
            sr = cr * qr + ci * qi
            si = ci * qr - cr * qi
            first = (rr * sr + ri * si, ri * sr - rr * si, sr * sr + si * si)
            second = (rr * dr + ri * di, rr * di - ri * dr, dr * dr + di * di)
            for side, terms in enumerate((first, second)):
                for comp, term in enumerate(terms):
                    for half in range(2):
                        if half:
                            kept = jnp.where(upper[side], term, 0.0)
                        else:
                            kept = jnp.where(upper[side], 0.0, term)
                        hi, lo = split(kept)
                        o = half * 192 + comp * 32 + pol * 16
                        at = slice(side * ROWS + l, side * ROWS + l + n)
                        s_ref[o : o + 16, at] = hi
                        s_ref[o + 96 : o + 112, at] = lo


def wrap(v, n):
    return jnp.where(v >= n, v - n, v)


def kernel(
    coh, vis, pairs, jones, duals, pen, table,
    jones_out, duals_out,
    raw, vraw, jraw, draw, jwide, dwide, cown, jmsg, dual, C, J, U, J1, S2, g_ref, u_own, usend, j1send, s2send,
    coef, xbuf, zbuf, oh, gcat, acc, x0, x1, x2, x3, s0, s1, s2, s3,
    ssem, rsem, lsem, cs, cr,
):
    ch = lax.axis_index("chan")
    me = lax.axis_index("bl")
    y, x, c = me // 4, (me // 2) % 2, me % 2
    xl, z = ch // 8, ch % 8
    base = ch * GROUP
    ys = [y] + [wrap(y + d, 4) for d in (1, 2, 3)]
    to = [ys[o // 4] * 4 + (x, 1 - x)[(o // 2) % 2] * 2 + (c, 1 - c)[o % 2] for o in range(GROUP)]
    xpeer = ((1 - xl) * 8 + z) * GROUP + me
    zpeer = [(xl * 8 + wrap(z + o, 8)) * GROUP + me for o in range(8)]

    def fro(o):
        return wrap(y + 4 - o // 4, 4) * 4 + wrap(x + (o // 2) % 2, 2) * 2 + wrap(c + o % 2, 2)

    mine = [
        pltpu.make_async_copy(jones, jraw, lsem.at[2, 0]),
        pltpu.make_async_copy(duals, draw, lsem.at[2, 1]),
    ] + [
        pltpu.make_async_copy(
            src.at[:, pl.ds(128 * t, 128)], dst.at[pl.ds(t * deep, deep)], lsem.at[i, t]
        )
        for t in range(ROWS // 128)
        for i, (src, dst, deep) in enumerate(((coh, raw, 64 * GROUP), (vis, vraw, 4 * GROUP)))
    ]
    for copy in mine:
        copy.start()
    barrier = pltpu.get_barrier_semaphore()
    for peer in [base + to[o] for o in range(1, GROUP)] + [xpeer] + zpeer[1:]:
        pl.semaphore_signal(barrier, inc=1, device_id=peer, device_id_type=LOGICAL)

    lane = lax.broadcasted_iota(jnp.int32, (8, 128), 1) // OWN
    ids = pairs[...].astype(f32)
    ids = jnp.concatenate(
        [ids[side : side + 1, 128 * t : 128 * t + 128] for side in range(2) for t in range(4)], axis=0
    )
    mine[0].wait()
    mine[1].wait()
    jwide[:, 0:OWN] = jraw[...]
    dwide[:, 0:OWN] = draw[...]

    @pl.loop(0, GROUP)
    def _(f):
        for h in range(2):
            for src, dst in ((jwide, jmsg), (dwide, dual)):
                out = None
                for a in range(4):
                    part = src[pl.ds(f + (a * DIRS + 8 * h) * GROUP, 8, stride=GROUP), :]
                    part = pltpu.roll(part, OWN * a, 1) if a else part
                    out = part if out is None else jnp.where(lane == a, part, out)
                dst[f, 8 * h : 8 * h + 8] = out
        jmsg[f, 16:24] = ids

    def basis(f, b):
        return table[(base + f) * NPOLY + b]

    def fit(it, target):
        total = [jnp.zeros((DIRS, 128), f32) for _ in range(NPOLY)]
        for f in range(GROUP):
            value = target(f)
            for b in range(NPOLY):
                total[b] += basis(f, b) * value
        for b in range(NPOLY):
            coef[2 * it, b] = total[b]

    fit(0, lambda f: jmsg[f, 0:16] + dual[f])
    for copy in mine[2:]:
        copy.wait()

    @pl.loop(0, GROUP)
    def _(f):
        for t in range(ROWS // 128):
            at = slice(128 * t, 128 * t + 128)
            for k in range(0, 64, 8):
                cown[f, k : k + 8, at] = raw[pl.ds(f + (64 * t + k) * GROUP, 8, stride=GROUP)]
            cown[f, 64:68, at] = vraw[pl.ds(f + 4 * t * GROUP, 4, stride=GROUP)]

    C[me] = cown[me]
    J[me] = jmsg[me]
    pl.semaphore_wait(barrier, 23)

    def remote(kind, o, src, dst):
        return pltpu.make_async_remote_copy(
            src_ref=src, dst_ref=dst, send_sem=ssem.at[kind, o], recv_sem=rsem.at[kind, o],
            device_id=base + to[o] if isinstance(o, int) else base, device_id_type=LOGICAL,
        )

    def jones_to(o):
        return remote(0, o, jmsg.at[to[o]], J.at[me])

    def coh_to(o):
        return remote(1, o, cown.at[to[o]], C.at[me])

    def coh_from(o):
        return remote(1, o, cown.at[0], C.at[0])

    def u_to(o):
        return remote(2, o, usend.at[to[o]], U.at[me])

    def j1_to(o):
        return remote(3, o, j1send.at[to[o]], J1.at[me])

    def s2_to(o):
        return remote(4, o, s2send.at[to[o]], S2.at[me])

    def x_copy(it):
        return pltpu.make_async_remote_copy(
            src_ref=coef.at[2 * it], dst_ref=xbuf.at[it], send_sem=cs.at[it, 0], recv_sem=cr.at[it, 0],
            device_id=xpeer, device_id_type=LOGICAL,
        )

    def z_copy(it, o):
        return pltpu.make_async_remote_copy(
            src_ref=coef.at[2 * it + 1], dst_ref=zbuf.at[it, o], send_sem=cs.at[it, o], recv_sem=cr.at[it, o],
            device_id=zpeer[o], device_id_type=LOGICAL,
        )

    def fit_x(it):
        x_copy(it).wait_recv()
        coef[2 * it + 1] = coef[2 * it] + xbuf[it]
        for o in ZORDER:
            z_copy(it, o).start()

    def fit_z(it):
        for o in ZORDER:
            z_copy(it, o).wait_recv()
        total = [coef[2 * it + 1, b] for b in range(NPOLY)]
        for o in range(1, 8):
            for b in range(NPOLY):
                total[b] += zbuf[it, o, b]
        return lambda f: sum(basis(f, b) * total[b] for b in range(NPOLY))

    x_copy(0).start()
    for o in range(1, GROUP):
        jones_to(o).start()
    for o in range(1, 8):
        coh_to(o).start()
    fit_x(0)
    for o in range(8, GROUP):
        coh_to(o).start()
    acc[...] = jnp.zeros_like(acc)
    for o in range(1, GROUP):
        jones_to(o).wait_recv()

    for q in range(4):
        for a, block in enumerate(regroup([J[4 * q + i, 0:16] for i in range(4)])):
            g_ref[16 * a : 16 * a + 16, 128 * q : 128 * q + 128] = block
    set_table(g_ref, gcat)

    @pl.loop(0, GROUP)
    def _(b):
        build_onehot(J, oh, b)

    @pl.loop(0, GROUP)
    def _(o):
        b = fro(o)

        @pl.when(o == 7)
        def _():
            fitted = fit_z(0)
            for f in range(GROUP):
                u = fitted(f) - dual[f]
                u_own[f] = u
                usend[f] = u
            U[me] = u_own[me]
            for o in range(1, GROUP):
                u_to(o).start()

        @pl.when(o > 0)
        def _():
            coh_from(o).wait_recv()

        x0[...] = jnp.dot(gcat[...], oh[b], preferred_element_type=f32)
        row_terms(C, J, x0, s0, b)
        acc[...] += lax.dot_general(
            s0[...], oh[b], (((1,), (1,)), ((), ())), preferred_element_type=f32
        )

    def sums(comp, pol, q):
        o, at = (q // 2) * 192 + comp * 32 + pol * 16, slice((q % 2) * 128, (q % 2) * 128 + 128)
        return acc[o : o + 16, at] + acc[o + 96 : o + 112, at]

    row = lax.broadcasted_iota(jnp.int32, (DIRS, 128), 0)
    weight = jnp.zeros((DIRS, 128), f32)
    for k in range(DIRS):
        weight = jnp.where(row == k, pen[k], weight)

    for o in range(1, GROUP):
        u_to(o).wait_recv()

    for q in range(4):
        u = regroup([U[4 * q + i] for i in range(4)])
        wide = [sums(2, pol, q) + weight for pol in range(2)]
        new = []
        for a in range(4):
            gain = g_ref[16 * a : 16 * a + 16, 128 * q : 128 * q + 128]
            gain = gain + (sums(a // 2, a % 2, q) + weight * (u[a] - gain)) / wide[a % 2]
            g_ref[16 * a : 16 * a + 16, 128 * q : 128 * q + 128] = gain
            new.append(gain)
        for i, slab in enumerate(regroup(new)):
            j1send[4 * q + i] = slab
    for o in range(1, GROUP):
        j1_to(o).start()
    J1[me] = j1send[me]
    set_table(g_ref, gcat)
    acc[...] = jnp.zeros_like(acc)

    @pl.loop(0, 4)
    def _(i):
        @pl.when(i == 2)
        def _():
            for o in range(1, GROUP):
                j1_to(o).wait_recv()
            fit(1, lambda f: 2.0 * J1[f] - u_own[f])
            x_copy(1).start()

        @pl.when(i == 3)
        def _():
            fit_x(1)

        for k, xs in enumerate((x0, x1, x2, x3)):
            xs[...] = jnp.dot(gcat[...], oh[4 * i + k], preferred_element_type=f32)
        for k, (xs, ss) in enumerate(((x0, s0), (x1, s1), (x2, s2), (x3, s3))):
            row_terms(C, J, xs, ss, 4 * i + k)
        total = acc[...]
        for k, ss in enumerate((s0, s1, s2, s3)):
            total += lax.dot_general(
                ss[...], oh[4 * i + k], (((1,), (1,)), ((), ())), preferred_element_type=f32
            )
        acc[...] = total

    for q in range(4):
        grads = regroup([sums(a // 2, a % 2, q) for a in range(4)])
        wides = [sums(2, pol, q) for pol in range(2)]
        wides = regroup([wides[a % 2][8 * (a // 2) : 8 * (a // 2) + 8] for a in range(4)])
        for i in range(4):
            s2send[4 * q + i, 0:16] = grads[i]
            s2send[4 * q + i, 16:24] = wides[i]
    for o in range(1, GROUP):
        s2_to(o).start()
    S2[me] = s2send[me]

    fitted = fit_z(1)
    for f in range(GROUP):
        u_own[f] = fitted(f) - (J1[f] - u_own[f])
    for o in range(1, GROUP):
        s2_to(o).wait_recv()

    low = lane < 2

    @pl.loop(0, GROUP)
    def _(f):
        packed = S2[f, 16:24]
        turned = pltpu.roll(packed, 64, 1)
        for h, wide in enumerate((jnp.where(low, packed, turned), jnp.where(low, turned, packed))):
            at = slice(8 * h, 8 * h + 8)
            gain, u, pk = J1[f, at], u_own[f, at], weight[at]
            gain = gain + (S2[f, at] + pk * (u - gain)) / (wide + pk)
            for value, dst in ((gain, jones_out), (gain - u, duals_out)):
                for a in range(4):
                    part = pltpu.roll(value, 128 - OWN * a, 1) if a else value
                    dst[pl.ds(f + (a * DIRS + 8 * h) * GROUP, 8, stride=GROUP), :] = part

    for o in range(1, GROUP):
        for copy in (jones_to, coh_to, u_to, j1_to, s2_to):
            copy(o).wait_send()
    for it in range(2):
        x_copy(it).wait_send()
        for o in ZORDER:
            z_copy(it, o).wait_send()


def body(visibility, coherency, station_pairs, jones_gains, scaled_duals, penalty):
    state = jones_gains.shape
    wide = jax.ShapeDtypeStruct((64 * GROUP, 128), f32)
    slab = (GROUP, DIRS, 128)
    msg = (GROUP, DIRS + 8, 128)
    hbm, vmem, smem = [
        pl.BlockSpec(memory_space=space) for space in (pltpu.HBM, pltpu.VMEM, pltpu.SMEM)
    ]
    outs = pl.pallas_call(
        kernel,
        out_shape=(wide, wide),
        in_specs=[hbm, hbm, vmem, hbm, hbm, smem, smem],
        out_specs=(vmem, vmem),
        scratch_shapes=[
            pltpu.VMEM((4 * 64 * GROUP, 128), f32),
            pltpu.VMEM((4 * 4 * GROUP, 128), f32),
            pltpu.VMEM((64 * GROUP, OWN), f32),
            pltpu.VMEM((64 * GROUP, OWN), f32),
            pltpu.VMEM((64 * GROUP, 128), f32),
            pltpu.VMEM((64 * GROUP, 128), f32),
            pltpu.VMEM((GROUP, 68, ROWS), f32),
            pltpu.VMEM(msg, f32),
            pltpu.VMEM(slab, f32),
            pltpu.VMEM((GROUP, 68, ROWS), f32),
            pltpu.VMEM(msg, f32),
            pltpu.VMEM(slab, f32),
            pltpu.VMEM(slab, f32),
            pltpu.VMEM(msg, f32),
            pltpu.VMEM((64, STATIONS), f32),
            pltpu.VMEM(slab, f32),
            pltpu.VMEM(slab, f32),
            pltpu.VMEM(slab, f32),
            pltpu.VMEM(msg, f32),
            pltpu.VMEM((4, NPOLY, DIRS, 128), f32),
            pltpu.VMEM((2, NPOLY, DIRS, 128), f32),
            pltpu.VMEM((2, 8, NPOLY, DIRS, 128), f32),
            pltpu.VMEM((GROUP, HALF, 2 * ROWS), bf16),
            pltpu.VMEM((256, HALF), bf16),
            pltpu.VMEM((384, HALF), f32),
        ]
        + [pltpu.VMEM((256, 2 * ROWS), f32)] * 4
        + [pltpu.VMEM((384, 2 * ROWS), bf16)] * 4
        + [
            pltpu.SemaphoreType.DMA((5, GROUP)),
            pltpu.SemaphoreType.DMA((5, GROUP)),
            pltpu.SemaphoreType.DMA((3, 4)),
            pltpu.SemaphoreType.DMA((2, 8)),
            pltpu.SemaphoreType.DMA((2, 8)),
        ],
        compiler_params=pltpu.CompilerParams(
            collective_id=0, has_side_effects=True, vmem_limit_bytes=56 * 2**20
        ),
    )(
        coherency.reshape(64 * GROUP, ROWS),
        visibility.reshape(4 * GROUP, ROWS),
        station_pairs,
        jones_gains.reshape(64 * GROUP, OWN),
        scaled_duals.reshape(64 * GROUP, OWN),
        penalty,
        jnp.asarray(cosine_table().reshape(-1)),
    )
    return tuple(out[:, :OWN].reshape(state) for out in outs)


def solution(mesh):
    state = P(None, None, None, "chan", "bl")
    return jax.shard_map(
        body,
        mesh=mesh,
        in_specs=(P(None, None, "chan", "bl"), state, P(None, "bl"), state, state, P()),
        out_specs=(state, state),
        check_vma=False,
    )
```

```python
import functools
import math

import jax
import jax.numpy as jnp
import numpy as np
from jax import lax
from jax.experimental import pallas as pl
from jax.experimental.pallas import tpu as pltpu
from jax.sharding import PartitionSpec as P

STATIONS = 512
CHANNELS = 256
NPOLY = 3
DIRS = 16
GROUP = 16
ROWS = 512
OWN = STATIONS // GROUP
HALF = 256
LOGICAL = pl.DeviceIdType.LOGICAL
ZORDER = (1, 7, 2, 6, 3, 5, 4)
FIRST, AMID, PAIR, USEND = 3, 8, 2, 4
f32, bf16 = jnp.float32, jnp.bfloat16


def cosine_table():
    freq = np.arange(CHANNELS, dtype=np.float64)[:, None]
    order = np.arange(NPOLY, dtype=np.float64)[None, :]
    scale = np.where(order < 0.5, math.sqrt(1.0 / CHANNELS), math.sqrt(2.0 / CHANNELS))
    return (scale * np.cos(math.pi * order * (freq + 0.5) / CHANNELS)).astype(np.float32)


def split(x):
    hi = x.astype(bf16)
    return hi, (x - hi.astype(f32)).astype(bf16)


def regroup(blocks):
    lane = lax.broadcasted_iota(jnp.int32, blocks[0].shape, 1) // OWN
    outs = []
    for i in range(4):
        out = None
        for a, block in enumerate(blocks):
            shift = (OWN * (a - i)) % 128
            moved = pltpu.roll(block, shift, 1) if shift else block
            out = moved if out is None else jnp.where(lane == a, moved, out)
        outs.append(out)
    return outs


def build_onehot(j_ref, oh_ref, b):
    station = lax.broadcasted_iota(jnp.int32, (HALF, 128), 0).astype(f32)
    for k in range(8):
        pair = j_ref[b, DIRS + k : DIRS + k + 1, :]
        low = jnp.where(pair >= HALF, pair - HALF, pair)
        oh_ref[b, :, 128 * k : 128 * k + 128] = jnp.where(station == low, 1.0, 0.0).astype(bf16)


def set_table(g_ref, gcat_ref):
    for row in range(0, 64, 16):
        for half in range(2):
            hi, lo = split(g_ref[row : row + 16, half * HALF : (half + 1) * HALF])
            gcat_ref[half * 128 + row : half * 128 + row + 16, :] = hi
            gcat_ref[half * 128 + 64 + row : half * 128 + 80 + row, :] = lo


def row_terms(c_ref, j_ref, x_ref, s_ref, b, n=128):
    for l in range(0, ROWS, n):
        upper = [
            jnp.broadcast_to(j_ref[b, pl.ds(DIRS + 4 * side + l // n, 1), :] >= HALF, (DIRS, n))
            for side in range(2)
        ]
        for pol in range(2):

            def gain(side, part):
                o = part * 32 + pol * 16
                at = slice(side * ROWS + l, side * ROWS + l + n)
                h0, l0, h1, l1 = [x_ref[k + o : k + o + 16, at] for k in (0, 64, 128, 192)]
                return jnp.where(upper[side], h1, h0) + jnp.where(upper[side], l1, l0)

            pr, pi, qr, qi = gain(0, 0), gain(0, 1), gain(1, 0), gain(1, 1)
            cr = c_ref[b, l // 2 + 16 * pol : l // 2 + 16 * pol + 16, :]
            ci = c_ref[b, l // 2 + 32 + 16 * pol : l // 2 + 48 + 16 * pol, :]
            dr = pr * cr - pi * ci
            di = pr * ci + pi * cr
            mr = dr * qr + di * qi
            mi = di * qr - dr * qi
            v = 256 + l // 32 + pol
            rr = c_ref[b, v : v + 1, :] - jnp.sum(mr, axis=0, keepdims=True)
            ri = c_ref[b, v + 2 : v + 3, :] - jnp.sum(mi, axis=0, keepdims=True)
            sr = cr * qr + ci * qi
            si = ci * qr - cr * qi
            first = (rr * sr + ri * si, ri * sr - rr * si, sr * sr + si * si)
            second = (rr * dr + ri * di, rr * di - ri * dr, dr * dr + di * di)
            for side, terms in enumerate((first, second)):
                for comp, term in enumerate(terms):
                    for half in range(2):
                        if half:
                            kept = jnp.where(upper[side], term, 0.0)
                        else:
                            kept = jnp.where(upper[side], 0.0, term)
                        hi, lo = split(kept)
                        o = half * 192 + comp * 32 + pol * 16
                        at = slice(side * ROWS + l, side * ROWS + l + n)
                        s_ref[o : o + 16, at] = hi
                        s_ref[o + 96 : o + 112, at] = lo


def wrap(v, n):
    return jnp.where(v >= n, v - n, v)


def turn(p):
    return (GROUP - p) % GROUP


ORDER = [turn(p) for p in range(GROUP)]


def kernel(
    coh, vis, pairs, jones, duals, pen, table,
    jones_out, duals_out,
    raw, vraw, jraw, draw, jwide, dwide, cown, jmsg, dual, C, J, U, J1, S2, g_ref, u_own, usend, j1send, s2send,
    coef, xbuf, zbuf, oh, gcat, acc, x0, x1, x2, x3, s0, s1, s2, s3,
    ssem, rsem, lsem, cs, cr,
):
    ch = lax.axis_index("chan")
    me = lax.axis_index("bl")
    y, x, c = me // 4, (me // 2) % 2, me % 2
    xl, z = ch // 8, ch % 8
    base = ch * GROUP
    ys = [y] + [wrap(y + d, 4) for d in (1, 2, 3)]
    to = [ys[o // 4] * 4 + (x, 1 - x)[(o // 2) % 2] * 2 + (c, 1 - c)[o % 2] for o in range(GROUP)]
    xpeer = ((1 - xl) * 8 + z) * GROUP + me
    zpeer = [(xl * 8 + wrap(z + o, 8)) * GROUP + me for o in range(8)]

    def fro(o):
        return wrap(y + 4 - o // 4, 4) * 4 + wrap(x + (o // 2) % 2, 2) * 2 + wrap(c + o % 2, 2)

    mine = [
        pltpu.make_async_copy(jones, jraw, lsem.at[2, 0]),
        pltpu.make_async_copy(duals, draw, lsem.at[2, 1]),
    ] + [
        pltpu.make_async_copy(
            src.at[:, pl.ds(128 * t, 128)], dst.at[pl.ds(t * deep, deep)], lsem.at[i, t]
        )
        for t in range(ROWS // 128)
        for i, (src, dst, deep) in enumerate(((coh, raw, 64 * GROUP), (vis, vraw, 4 * GROUP)))
    ]
    for copy in mine:
        copy.start()
    barrier = pltpu.get_barrier_semaphore()
    for peer in [base + to[o] for o in range(1, GROUP)] + [xpeer] + zpeer[1:]:
        pl.semaphore_signal(barrier, inc=1, device_id=peer, device_id_type=LOGICAL)

    lane = lax.broadcasted_iota(jnp.int32, (8, 128), 1) // OWN
    ids = pairs[...].astype(f32)
    ids = jnp.concatenate(
        [ids[side : side + 1, 128 * t : 128 * t + 128] for side in range(2) for t in range(4)], axis=0
    )
    def relay(f):
        for t in range(ROWS // 128):
            for k in range(64 * t, 64 * t + 64, 8):
                cown[f, k : k + 8] = raw[pl.ds(f + k * GROUP, 8, stride=GROUP)]
            cown[f, 256 + 4 * t : 260 + 4 * t] = vraw[pl.ds(f + 4 * t * GROUP, 4, stride=GROUP)]

    def basis(f, b):
        return table[(base + f) * NPOLY + b]

    def fit(it, target):
        total = [jnp.zeros((DIRS, 128), f32) for _ in range(NPOLY)]
        for f in range(GROUP):
            value = target(f)
            for b in range(NPOLY):
                total[b] += basis(f, b) * value
        for b in range(NPOLY):
            coef[2 * it, b] = total[b]

    def remote(kind, o, src, dst):
        return pltpu.make_async_remote_copy(
            src_ref=src, dst_ref=dst, send_sem=ssem.at[kind, o], recv_sem=rsem.at[kind, o],
            device_id=base + to[o] if isinstance(o, int) else base, device_id_type=LOGICAL,
        )

    def jones_to(o):
        return remote(0, o, jmsg.at[to[o]], J.at[me])

    def coh_to(o):
        return remote(1, o, cown.at[to[o]], C.at[me])

    def coh_from(o):
        return remote(1, o, cown.at[0], C.at[0])

    def u_to(o):
        return remote(2, o, usend.at[to[o]], U.at[me])

    def j1_to(o):
        return remote(3, o, j1send.at[to[o]], J1.at[me])

    def s2_to(o):
        return remote(4, o, s2send.at[to[o]], S2.at[me])

    def x_copy(it):
        return pltpu.make_async_remote_copy(
            src_ref=coef.at[2 * it], dst_ref=xbuf.at[it], send_sem=cs.at[it, 0], recv_sem=cr.at[it, 0],
            device_id=xpeer, device_id_type=LOGICAL,
        )

    def z_copy(it, o):
        return pltpu.make_async_remote_copy(
            src_ref=coef.at[2 * it + 1], dst_ref=zbuf.at[it, o], send_sem=cs.at[it, o], recv_sem=cr.at[it, o],
            device_id=zpeer[o], device_id_type=LOGICAL,
        )

    def fit_x(it):
        x_copy(it).wait_recv()
        coef[2 * it + 1] = coef[2 * it] + xbuf[it]
        for o in ZORDER:
            z_copy(it, o).start()

    def fit_z(it):
        for o in ZORDER:
            z_copy(it, o).wait_recv()
        total = [coef[2 * it + 1, b] for b in range(NPOLY)]
        for o in range(1, 8):
            for b in range(NPOLY):
                total[b] += zbuf[it, o, b]
        return lambda f: sum(basis(f, b) * total[b] for b in range(NPOLY))

    for copy in mine[2:]:
        copy.wait()
    for p in range(1, FIRST):
        relay(to[ORDER[p]])
    pl.semaphore_wait(barrier, 23)
    for p in range(1, FIRST):
        coh_to(ORDER[p]).start()

    mine[0].wait()
    mine[1].wait()
    jwide[:, 0:OWN] = jraw[...]
    dwide[:, 0:OWN] = draw[...]

    @pl.loop(0, GROUP)
    def _(f):
        for h in range(2):
            for src, dst in ((jwide, jmsg), (dwide, dual)):
                out = None
                for a in range(4):
                    part = src[pl.ds(f + (a * DIRS + 8 * h) * GROUP, 8, stride=GROUP), :]
                    part = pltpu.roll(part, OWN * a, 1) if a else part
                    out = part if out is None else jnp.where(lane == a, part, out)
                dst[f, 8 * h : 8 * h + 8] = out
        jmsg[f, 16:24] = ids

    fit(0, lambda f: jmsg[f, 0:16] + dual[f])
    x_copy(0).start()
    for o in range(1, GROUP):
        jones_to(o).start()
    for p in range(FIRST, AMID):
        relay(to[ORDER[p]])
        coh_to(ORDER[p]).start()
    J[me] = jmsg[me]
    for p in range(AMID, GROUP):
        relay(to[ORDER[p]])
    relay(me)
    C[me] = cown[me]
    acc[...] = jnp.zeros_like(acc)
    fit_x(0)
    for p in range(AMID, GROUP):
        coh_to(ORDER[p]).start()
    for o in range(1, GROUP):
        jones_to(o).wait_recv()

    for q in range(4):
        for a, block in enumerate(regroup([J[4 * q + i, 0:16] for i in range(4)])):
            g_ref[16 * a : 16 * a + 16, 128 * q : 128 * q + 128] = block
    set_table(g_ref, gcat)

    @pl.loop(0, GROUP)
    def _(b):
        build_onehot(J, oh, b)

    def rows(blocks):
        work = list(zip(blocks, (x0, x1, x2, x3), (s0, s1, s2, s3)))
        for b, xs, ss in work:
            xs[...] = jnp.dot(gcat[...], oh[b], preferred_element_type=f32)
        for b, xs, ss in work:
            row_terms(C, J, xs, ss, b)
        total = acc[...]
        for b, xs, ss in work:
            total += lax.dot_general(
                ss[...], oh[b], (((1,), (1,)), ((), ())), preferred_element_type=f32
            )
        acc[...] = total

    @pl.loop(0, GROUP // PAIR)
    def _(i):
        @pl.when(i == USEND)
        def _():
            fitted = fit_z(0)
            for f in range(GROUP):
                u = fitted(f) - dual[f]
                u_own[f] = u
                usend[f] = u
            U[me] = u_own[me]
            for o in range(1, GROUP):
                u_to(o).start()

        blocks = []
        for k in range(PAIR):
            p = PAIR * i + k
            o = turn(p)
            blocks.append(fro(o))
            if k:
                coh_from(o).wait_recv()
            else:

                @pl.when(p > 0)
                def _():
                    coh_from(o).wait_recv()

        rows(blocks)

    def sums(comp, pol, q):
        o, at = (q // 2) * 192 + comp * 32 + pol * 16, slice((q % 2) * 128, (q % 2) * 128 + 128)
        return acc[o : o + 16, at] + acc[o + 96 : o + 112, at]

    row = lax.broadcasted_iota(jnp.int32, (DIRS, 128), 0)
    weight = jnp.zeros((DIRS, 128), f32)
    for k in range(DIRS):
        weight = jnp.where(row == k, pen[k], weight)

    for o in range(1, GROUP):
        u_to(o).wait_recv()

    for q in range(4):
        u = regroup([U[4 * q + i] for i in range(4)])
        wide = [sums(2, pol, q) + weight for pol in range(2)]
        new = []
        for a in range(4):
            gain = g_ref[16 * a : 16 * a + 16, 128 * q : 128 * q + 128]
            gain = gain + (sums(a // 2, a % 2, q) + weight * (u[a] - gain)) / wide[a % 2]
            g_ref[16 * a : 16 * a + 16, 128 * q : 128 * q + 128] = gain
            new.append(gain)
        for i, slab in enumerate(regroup(new)):
            j1send[4 * q + i] = slab
    for o in range(1, GROUP):
        j1_to(o).start()
    J1[me] = j1send[me]
    set_table(g_ref, gcat)
    acc[...] = jnp.zeros_like(acc)

    @pl.loop(0, 4)
    def _(i):
        @pl.when(i == 2)
        def _():
            for o in range(1, GROUP):
                j1_to(o).wait_recv()
            fit(1, lambda f: 2.0 * J1[f] - u_own[f])
            x_copy(1).start()

        @pl.when(i == 3)
        def _():
            fit_x(1)

        rows([4 * i + k for k in range(4)])

    for q in range(4):
        grads = regroup([sums(a // 2, a % 2, q) for a in range(4)])
        wides = [sums(2, pol, q) for pol in range(2)]
        wides = regroup([wides[a % 2][8 * (a // 2) : 8 * (a // 2) + 8] for a in range(4)])
        for i in range(4):
            s2send[4 * q + i, 0:16] = grads[i]
            s2send[4 * q + i, 16:24] = wides[i]
    for o in range(1, GROUP):
        s2_to(o).start()
    S2[me] = s2send[me]

    fitted = fit_z(1)
    for f in range(GROUP):
        u_own[f] = fitted(f) - (J1[f] - u_own[f])
    for o in range(1, GROUP):
        s2_to(o).wait_recv()

    low = lane < 2

    @pl.loop(0, GROUP)
    def _(f):
        packed = S2[f, 16:24]
        turned = pltpu.roll(packed, 64, 1)
        for h, wide in enumerate((jnp.where(low, packed, turned), jnp.where(low, turned, packed))):
            at = slice(8 * h, 8 * h + 8)
            gain, u, pk = J1[f, at], u_own[f, at], weight[at]
            gain = gain + (S2[f, at] + pk * (u - gain)) / (wide + pk)
            jones_out[f, at] = gain
            duals_out[f, at] = gain - u

    for o in range(1, GROUP):
        for copy in (jones_to, coh_to, u_to, j1_to, s2_to):
            copy(o).wait_send()
    for it in range(2):
        x_copy(it).wait_send()
        for o in ZORDER:
            z_copy(it, o).wait_send()


def body(visibility, coherency, station_pairs, jones_gains, scaled_duals, penalty):
    slab = (GROUP, DIRS, 128)
    packed = jax.ShapeDtypeStruct(slab, f32)
    msg = (GROUP, DIRS + 8, 128)
    hbm, vmem, smem = [
        pl.BlockSpec(memory_space=space) for space in (pltpu.HBM, pltpu.VMEM, pltpu.SMEM)
    ]
    packed = pl.pallas_call(
        kernel,
        out_shape=(packed, packed),
        in_specs=[hbm, hbm, vmem, hbm, hbm, smem, smem],
        out_specs=(vmem, vmem),
        scratch_shapes=[
            pltpu.VMEM((4 * 64 * GROUP, 128), f32),
            pltpu.VMEM((4 * 4 * GROUP, 128), f32),
            pltpu.VMEM((64 * GROUP, OWN), f32),
            pltpu.VMEM((64 * GROUP, OWN), f32),
            pltpu.VMEM((64 * GROUP, 128), f32),
            pltpu.VMEM((64 * GROUP, 128), f32),
            pltpu.VMEM((GROUP, 272, 128), f32),
            pltpu.VMEM(msg, f32),
            pltpu.VMEM(slab, f32),
            pltpu.VMEM((GROUP, 272, 128), f32),
            pltpu.VMEM(msg, f32),
            pltpu.VMEM(slab, f32),
            pltpu.VMEM(slab, f32),
            pltpu.VMEM(msg, f32),
            pltpu.VMEM((64, STATIONS), f32),
            pltpu.VMEM(slab, f32),
            pltpu.VMEM(slab, f32),
            pltpu.VMEM(slab, f32),
            pltpu.VMEM(msg, f32),
            pltpu.VMEM((4, NPOLY, DIRS, 128), f32),
            pltpu.VMEM((2, NPOLY, DIRS, 128), f32),
            pltpu.VMEM((2, 8, NPOLY, DIRS, 128), f32),
            pltpu.VMEM((GROUP, HALF, 2 * ROWS), bf16),
            pltpu.VMEM((256, HALF), bf16),
            pltpu.VMEM((384, HALF), f32),
        ]
        + [pltpu.VMEM((256, 2 * ROWS), f32)] * 4
        + [pltpu.VMEM((384, 2 * ROWS), bf16)] * 4
        + [
            pltpu.SemaphoreType.DMA((5, GROUP)),
            pltpu.SemaphoreType.DMA((5, GROUP)),
            pltpu.SemaphoreType.DMA((3, 4)),
            pltpu.SemaphoreType.DMA((2, 8)),
            pltpu.SemaphoreType.DMA((2, 8)),
        ],
        compiler_params=pltpu.CompilerParams(
            collective_id=0, has_side_effects=True, vmem_limit_bytes=56 * 2**20
        ),
    )(
        coherency.reshape(64 * GROUP, ROWS),
        visibility.reshape(4 * GROUP, ROWS),
        station_pairs,
        jones_gains.reshape(64 * GROUP, OWN),
        scaled_duals.reshape(64 * GROUP, OWN),
        penalty,
        jnp.asarray(cosine_table().reshape(-1)),
    )
    outs = [out.reshape(GROUP, DIRS, 2, 2, OWN) for out in packed]
    return tuple(jnp.transpose(out, (2, 3, 1, 0, 4)) for out in outs)


def solution(mesh):
    state = P(None, None, None, "chan", "bl")
    return jax.shard_map(
        body,
        mesh=mesh,
        in_specs=(P(None, None, "chan", "bl"), state, P(None, "bl"), state, state, P()),
        out_specs=(state, state),
        check_vma=False,
    )
```

```python
import functools
import math

import jax
import jax.numpy as jnp
import numpy as np
from jax import lax
from jax.experimental import pallas as pl
from jax.experimental.pallas import tpu as pltpu
from jax.sharding import PartitionSpec as P

STATIONS = 512
CHANNELS = 256
NPOLY = 3
DIRS = 16
GROUP = 16
ROWS = 512
OWN = STATIONS // GROUP
HALF = 256
LOGICAL = pl.DeviceIdType.LOGICAL
ZORDER = (1, 7, 2, 6, 3, 5, 4)
FIRST, AMID, PAIR, USEND = 3, 8, 4, 2
f32, bf16 = jnp.float32, jnp.bfloat16


def cosine_table():
    freq = np.arange(CHANNELS, dtype=np.float64)[:, None]
    order = np.arange(NPOLY, dtype=np.float64)[None, :]
    scale = np.where(order < 0.5, math.sqrt(1.0 / CHANNELS), math.sqrt(2.0 / CHANNELS))
    return (scale * np.cos(math.pi * order * (freq + 0.5) / CHANNELS)).astype(np.float32)


def split(x):
    hi = x.astype(bf16)
    return hi, (x - hi.astype(f32)).astype(bf16)


def regroup(blocks):
    lane = lax.broadcasted_iota(jnp.int32, blocks[0].shape, 1) // OWN
    outs = []
    for i in range(4):
        out = None
        for a, block in enumerate(blocks):
            shift = (OWN * (a - i)) % 128
            moved = pltpu.roll(block, shift, 1) if shift else block
            out = moved if out is None else jnp.where(lane == a, moved, out)
        outs.append(out)
    return outs


def build_onehot(j_ref, oh_ref, b):
    station = lax.broadcasted_iota(jnp.int32, (HALF, 128), 0).astype(f32)
    for k in range(8):
        pair = j_ref[b, DIRS + k : DIRS + k + 1, :]
        low = jnp.where(pair >= HALF, pair - HALF, pair)
        oh_ref[b, :, 128 * k : 128 * k + 128] = jnp.where(station == low, 1.0, 0.0).astype(bf16)


def set_table(g_ref, gcat_ref):
    for row in range(0, 64, 16):
        for half in range(2):
            hi, lo = split(g_ref[row : row + 16, half * HALF : (half + 1) * HALF])
            gcat_ref[half * 128 + row : half * 128 + row + 16, :] = hi
            gcat_ref[half * 128 + 64 + row : half * 128 + 80 + row, :] = lo


def row_terms(c_ref, j_ref, x_ref, s_ref, b, n=128):
    for l in range(0, ROWS, n):
        upper = [
            jnp.broadcast_to(j_ref[b, pl.ds(DIRS + 4 * side + l // n, 1), :] >= HALF, (DIRS, n))
            for side in range(2)
        ]
        for pol in range(2):

            def gain(side, part):
                o = part * 32 + pol * 16
                at = slice(side * ROWS + l, side * ROWS + l + n)
                h0, l0, h1, l1 = [x_ref[k + o : k + o + 16, at] for k in (0, 64, 128, 192)]
                return jnp.where(upper[side], h1, h0) + jnp.where(upper[side], l1, l0)

            pr, pi, qr, qi = gain(0, 0), gain(0, 1), gain(1, 0), gain(1, 1)
            cr = c_ref[b, l // 2 + 16 * pol : l // 2 + 16 * pol + 16, :]
            ci = c_ref[b, l // 2 + 32 + 16 * pol : l // 2 + 48 + 16 * pol, :]
            dr = pr * cr - pi * ci
            di = pr * ci + pi * cr
            mr = dr * qr + di * qi
            mi = di * qr - dr * qi
            v = 256 + l // 32 + pol
            rr = c_ref[b, v : v + 1, :] - jnp.sum(mr, axis=0, keepdims=True)
            ri = c_ref[b, v + 2 : v + 3, :] - jnp.sum(mi, axis=0, keepdims=True)
            sr = cr * qr + ci * qi
            si = ci * qr - cr * qi
            first = (rr * sr + ri * si, ri * sr - rr * si, sr * sr + si * si)
            second = (rr * dr + ri * di, rr * di - ri * dr, dr * dr + di * di)
            for side, terms in enumerate((first, second)):
                for comp, term in enumerate(terms):
                    for half in range(2):
                        if half:
                            kept = jnp.where(upper[side], term, 0.0)
                        else:
                            kept = jnp.where(upper[side], 0.0, term)
                        hi, lo = split(kept)
                        o = half * 192 + comp * 32 + pol * 16
                        at = slice(side * ROWS + l, side * ROWS + l + n)
                        s_ref[o : o + 16, at] = hi
                        s_ref[o + 96 : o + 112, at] = lo


def wrap(v, n):
    return jnp.where(v >= n, v - n, v)


def turn(p):
    return (GROUP - p) % GROUP


ORDER = [turn(p) for p in range(GROUP)]


def kernel(
    coh, vis, pairs, jones, duals, pen, table,
    jones_out, duals_out,
    raw, vraw, jraw, draw, jwide, dwide, cown, jmsg, dual, C, J, U, J1, S2, g_ref, u_own, usend, j1send, s2send,
    coef, xbuf, zbuf, oh, gcat, acc, x0, x1, x2, x3, s0, s1, s2, s3,
    ssem, rsem, lsem, cs, cr,
):
    ch = lax.axis_index("chan")
    me = lax.axis_index("bl")
    y, x, c = me // 4, (me // 2) % 2, me % 2
    xl, z = ch // 8, ch % 8
    base = ch * GROUP
    ys = [y] + [wrap(y + d, 4) for d in (1, 2, 3)]
    to = [ys[o // 4] * 4 + (x, 1 - x)[(o // 2) % 2] * 2 + (c, 1 - c)[o % 2] for o in range(GROUP)]
    xpeer = ((1 - xl) * 8 + z) * GROUP + me
    zpeer = [(xl * 8 + wrap(z + o, 8)) * GROUP + me for o in range(8)]

    def fro(o):
        return wrap(y + 4 - o // 4, 4) * 4 + wrap(x + (o // 2) % 2, 2) * 2 + wrap(c + o % 2, 2)

    mine = [
        pltpu.make_async_copy(jones, jraw, lsem.at[2, 0]),
        pltpu.make_async_copy(duals, draw, lsem.at[2, 1]),
    ] + [
        pltpu.make_async_copy(
            src.at[:, pl.ds(128 * t, 128)], dst.at[pl.ds(t * deep, deep)], lsem.at[i, t]
        )
        for t in range(ROWS // 128)
        for i, (src, dst, deep) in enumerate(((coh, raw, 64 * GROUP), (vis, vraw, 4 * GROUP)))
    ]
    for copy in mine:
        copy.start()
    barrier = pltpu.get_barrier_semaphore()
    for peer in [base + to[o] for o in range(1, GROUP)] + [xpeer] + zpeer[1:]:
        pl.semaphore_signal(barrier, inc=1, device_id=peer, device_id_type=LOGICAL)

    lane = lax.broadcasted_iota(jnp.int32, (8, 128), 1) // OWN
    ids = pairs[...].astype(f32)
    ids = jnp.concatenate(
        [ids[side : side + 1, 128 * t : 128 * t + 128] for side in range(2) for t in range(4)], axis=0
    )
    def relay(f):
        for t in range(ROWS // 128):
            for k in range(64 * t, 64 * t + 64, 8):
                cown[f, k : k + 8] = raw[pl.ds(f + k * GROUP, 8, stride=GROUP)]
            cown[f, 256 + 4 * t : 260 + 4 * t] = vraw[pl.ds(f + 4 * t * GROUP, 4, stride=GROUP)]

    def basis(f, b):
        return table[(base + f) * NPOLY + b]

    def fit(it, target):
        total = [jnp.zeros((DIRS, 128), f32) for _ in range(NPOLY)]
        for f in range(GROUP):
            value = target(f)
            for b in range(NPOLY):
                total[b] += basis(f, b) * value
        for b in range(NPOLY):
            coef[2 * it, b] = total[b]

    def remote(kind, o, src, dst):
        return pltpu.make_async_remote_copy(
            src_ref=src, dst_ref=dst, send_sem=ssem.at[kind, o], recv_sem=rsem.at[kind, o],
            device_id=base + to[o] if isinstance(o, int) else base, device_id_type=LOGICAL,
        )

    def jones_to(o):
        return remote(0, o, jmsg.at[to[o]], J.at[me])

    def coh_to(o):
        return remote(1, o, cown.at[to[o]], C.at[me])

    def coh_from(o):
        return remote(1, o, cown.at[0], C.at[0])

    def u_to(o):
        return remote(2, o, usend.at[to[o]], U.at[me])

    def j1_to(o):
        return remote(3, o, j1send.at[to[o]], J1.at[me])

    def s2_to(o):
        return remote(4, o, s2send.at[to[o]], S2.at[me])

    def x_copy(it):
        return pltpu.make_async_remote_copy(
            src_ref=coef.at[2 * it], dst_ref=xbuf.at[it], send_sem=cs.at[it, 0], recv_sem=cr.at[it, 0],
            device_id=xpeer, device_id_type=LOGICAL,
        )

    def z_copy(it, o):
        return pltpu.make_async_remote_copy(
            src_ref=coef.at[2 * it + 1], dst_ref=zbuf.at[it, o], send_sem=cs.at[it, o], recv_sem=cr.at[it, o],
            device_id=zpeer[o], device_id_type=LOGICAL,
        )

    def fit_x(it):
        x_copy(it).wait_recv()
        coef[2 * it + 1] = coef[2 * it] + xbuf[it]
        for o in ZORDER:
            z_copy(it, o).start()

    def fit_z(it):
        for o in ZORDER:
            z_copy(it, o).wait_recv()
        total = [coef[2 * it + 1, b] for b in range(NPOLY)]
        for o in range(1, 8):
            for b in range(NPOLY):
                total[b] += zbuf[it, o, b]
        return lambda f: sum(basis(f, b) * total[b] for b in range(NPOLY))

    for copy in mine[2:]:
        copy.wait()
    for p in range(1, FIRST):
        relay(to[ORDER[p]])
    pl.semaphore_wait(barrier, 23)
    for p in range(1, FIRST):
        coh_to(ORDER[p]).start()

    mine[0].wait()
    mine[1].wait()
    jwide[:, 0:OWN] = jraw[...]
    dwide[:, 0:OWN] = draw[...]

    @pl.loop(0, GROUP)
    def _(f):
        for h in range(2):
            for src, dst in ((jwide, jmsg), (dwide, dual)):
                out = None
                for a in range(4):
                    part = src[pl.ds(f + (a * DIRS + 8 * h) * GROUP, 8, stride=GROUP), :]
                    part = pltpu.roll(part, OWN * a, 1) if a else part
                    out = part if out is None else jnp.where(lane == a, part, out)
                dst[f, 8 * h : 8 * h + 8] = out
        jmsg[f, 16:24] = ids

    fit(0, lambda f: jmsg[f, 0:16] + dual[f])
    x_copy(0).start()
    for o in range(1, GROUP):
        jones_to(o).start()
    for p in range(FIRST, AMID):
        relay(to[ORDER[p]])
        coh_to(ORDER[p]).start()
    J[me] = jmsg[me]
    for p in range(AMID, GROUP):
        relay(to[ORDER[p]])
    relay(me)
    C[me] = cown[me]
    acc[...] = jnp.zeros_like(acc)
    fit_x(0)
    for p in range(AMID, GROUP):
        coh_to(ORDER[p]).start()
    for o in range(1, GROUP):
        jones_to(o).wait_recv()

    for q in range(4):
        for a, block in enumerate(regroup([J[4 * q + i, 0:16] for i in range(4)])):
            g_ref[16 * a : 16 * a + 16, 128 * q : 128 * q + 128] = block
    set_table(g_ref, gcat)

    @pl.loop(0, GROUP)
    def _(b):
        build_onehot(J, oh, b)

    def rows(blocks):
        work = list(zip(blocks, (x0, x1, x2, x3), (s0, s1, s2, s3)))
        for b, xs, ss in work:
            xs[...] = jnp.dot(gcat[...], oh[b], preferred_element_type=f32)
        for b, xs, ss in work:
            row_terms(C, J, xs, ss, b)
        total = acc[...]
        for b, xs, ss in work:
            total += lax.dot_general(
                ss[...], oh[b], (((1,), (1,)), ((), ())), preferred_element_type=f32
            )
        acc[...] = total

    @pl.loop(0, GROUP // PAIR)
    def _(i):
        @pl.when(i == USEND)
        def _():
            fitted = fit_z(0)
            for f in range(GROUP):
                u = fitted(f) - dual[f]
                u_own[f] = u
                usend[f] = u
            U[me] = u_own[me]
            for o in range(1, GROUP):
                u_to(o).start()

        blocks = []
        for k in range(PAIR):
            p = PAIR * i + k
            o = turn(p)
            blocks.append(fro(o))
            if k:
                coh_from(o).wait_recv()
            else:

                @pl.when(p > 0)
                def _():
                    coh_from(o).wait_recv()

        rows(blocks)

    def sums(comp, pol, q):
        o, at = (q // 2) * 192 + comp * 32 + pol * 16, slice((q % 2) * 128, (q % 2) * 128 + 128)
        return acc[o : o + 16, at] + acc[o + 96 : o + 112, at]

    row = lax.broadcasted_iota(jnp.int32, (DIRS, 128), 0)
    weight = jnp.zeros((DIRS, 128), f32)
    for k in range(DIRS):
        weight = jnp.where(row == k, pen[k], weight)

    for o in range(1, GROUP):
        u_to(o).wait_recv()

    for q in range(4):
        u = regroup([U[4 * q + i] for i in range(4)])
        wide = [sums(2, pol, q) + weight for pol in range(2)]
        new = []
        for a in range(4):
            gain = g_ref[16 * a : 16 * a + 16, 128 * q : 128 * q + 128]
            gain = gain + (sums(a // 2, a % 2, q) + weight * (u[a] - gain)) / wide[a % 2]
            g_ref[16 * a : 16 * a + 16, 128 * q : 128 * q + 128] = gain
            new.append(gain)
        for i, slab in enumerate(regroup(new)):
            j1send[4 * q + i] = slab
    for o in range(1, GROUP):
        j1_to(o).start()
    J1[me] = j1send[me]
    set_table(g_ref, gcat)
    acc[...] = jnp.zeros_like(acc)

    @pl.loop(0, 4)
    def _(i):
        @pl.when(i == 2)
        def _():
            for o in range(1, GROUP):
                j1_to(o).wait_recv()
            fit(1, lambda f: 2.0 * J1[f] - u_own[f])
            x_copy(1).start()

        @pl.when(i == 3)
        def _():
            fit_x(1)

        rows([4 * i + k for k in range(4)])

    for q in range(4):
        grads = regroup([sums(a // 2, a % 2, q) for a in range(4)])
        wides = [sums(2, pol, q) for pol in range(2)]
        wides = regroup([wides[a % 2][8 * (a // 2) : 8 * (a // 2) + 8] for a in range(4)])
        for i in range(4):
            s2send[4 * q + i, 0:16] = grads[i]
            s2send[4 * q + i, 16:24] = wides[i]
    for o in range(1, GROUP):
        s2_to(o).start()
    S2[me] = s2send[me]

    fitted = fit_z(1)
    for f in range(GROUP):
        u_own[f] = fitted(f) - (J1[f] - u_own[f])
    for o in range(1, GROUP):
        s2_to(o).wait_recv()

    low = lane < 2

    @pl.loop(0, GROUP)
    def _(f):
        packed = S2[f, 16:24]
        turned = pltpu.roll(packed, 64, 1)
        for h, wide in enumerate((jnp.where(low, packed, turned), jnp.where(low, turned, packed))):
            at = slice(8 * h, 8 * h + 8)
            gain, u, pk = J1[f, at], u_own[f, at], weight[at]
            gain = gain + (S2[f, at] + pk * (u - gain)) / (wide + pk)
            jones_out[f, at] = gain
            duals_out[f, at] = gain - u

    for o in range(1, GROUP):
        for copy in (jones_to, coh_to, u_to, j1_to, s2_to):
            copy(o).wait_send()
    for it in range(2):
        x_copy(it).wait_send()
        for o in ZORDER:
            z_copy(it, o).wait_send()


def body(visibility, coherency, station_pairs, jones_gains, scaled_duals, penalty):
    slab = (GROUP, DIRS, 128)
    packed = jax.ShapeDtypeStruct(slab, f32)
    msg = (GROUP, DIRS + 8, 128)
    hbm, vmem, smem = [
        pl.BlockSpec(memory_space=space) for space in (pltpu.HBM, pltpu.VMEM, pltpu.SMEM)
    ]
    packed = pl.pallas_call(
        kernel,
        out_shape=(packed, packed),
        in_specs=[hbm, hbm, vmem, hbm, hbm, smem, smem],
        out_specs=(vmem, vmem),
        scratch_shapes=[
            pltpu.VMEM((4 * 64 * GROUP, 128), f32),
            pltpu.VMEM((4 * 4 * GROUP, 128), f32),
            pltpu.VMEM((64 * GROUP, OWN), f32),
            pltpu.VMEM((64 * GROUP, OWN), f32),
            pltpu.VMEM((64 * GROUP, 128), f32),
            pltpu.VMEM((64 * GROUP, 128), f32),
            pltpu.VMEM((GROUP, 272, 128), f32),
            pltpu.VMEM(msg, f32),
            pltpu.VMEM(slab, f32),
            pltpu.VMEM((GROUP, 272, 128), f32),
            pltpu.VMEM(msg, f32),
            pltpu.VMEM(slab, f32),
            pltpu.VMEM(slab, f32),
            pltpu.VMEM(msg, f32),
            pltpu.VMEM((64, STATIONS), f32),
            pltpu.VMEM(slab, f32),
            pltpu.VMEM(slab, f32),
            pltpu.VMEM(slab, f32),
            pltpu.VMEM(msg, f32),
            pltpu.VMEM((4, NPOLY, DIRS, 128), f32),
            pltpu.VMEM((2, NPOLY, DIRS, 128), f32),
            pltpu.VMEM((2, 8, NPOLY, DIRS, 128), f32),
            pltpu.VMEM((GROUP, HALF, 2 * ROWS), bf16),
            pltpu.VMEM((256, HALF), bf16),
            pltpu.VMEM((384, HALF), f32),
        ]
        + [pltpu.VMEM((256, 2 * ROWS), f32)] * 4
        + [pltpu.VMEM((384, 2 * ROWS), bf16)] * 4
        + [
            pltpu.SemaphoreType.DMA((5, GROUP)),
            pltpu.SemaphoreType.DMA((5, GROUP)),
            pltpu.SemaphoreType.DMA((3, 4)),
            pltpu.SemaphoreType.DMA((2, 8)),
            pltpu.SemaphoreType.DMA((2, 8)),
        ],
        compiler_params=pltpu.CompilerParams(
            collective_id=0, has_side_effects=True, vmem_limit_bytes=56 * 2**20
        ),
    )(
        coherency.reshape(64 * GROUP, ROWS),
        visibility.reshape(4 * GROUP, ROWS),
        station_pairs,
        jones_gains.reshape(64 * GROUP, OWN),
        scaled_duals.reshape(64 * GROUP, OWN),
        penalty,
        jnp.asarray(cosine_table().reshape(-1)),
    )
    outs = [out.reshape(GROUP, DIRS, 2, 2, OWN) for out in packed]
    return tuple(jnp.transpose(out, (2, 3, 1, 0, 4)) for out in outs)


def solution(mesh):
    state = P(None, None, None, "chan", "bl")
    return jax.shard_map(
        body,
        mesh=mesh,
        in_specs=(P(None, None, "chan", "bl"), state, P(None, "bl"), state, state, P()),
        out_specs=(state, state),
        check_vma=False,
    )
```
